32 devices in a mesh: groups: 2 (over x), blk: 16 (over z, y, core).
Axes of the slice: x: 2, y: 2, z: 4, core: 2. Of those that a mesh axis runs over, the one named last changes fastest.
Arguments:
- points: bfloat16 [16384, 256], P(('groups', 'blk')), parts along dimension 0, may hold values from -6 to 6
- left_vec: bfloat16 [16384, 64], P(('groups', 'blk')), parts along dimension 0, may hold values from -6 to 6
- right_vec: bfloat16 [16384, 64], P(('groups', 'blk')), parts along dimension 0, may hold values from -6 to 6
Outputs:
- kernel_vu: float32 [16384, 128], P(('groups', 'blk')), parts along dimension 0
- feature_grad: float32 [16384, 256], P(('groups', 'blk')), parts along dimension 0
The draws below stay inside these ranges and needn't reach their ends.
There are 2 independent parts, one for each index of `groups`. The reference program is written for one: setup_inputs(seed, part) draws one part's arguments, and reference() takes and returns one part's arrays. A program takes and returns all parts, laid end to end along the dimension named above; each array names one. Nothing has to cross between parts.
All inputs are finite; a program needn't handle non-finite values.
Results may differ from the reference program's by a relative error of at most 0.0031.
Values may be sent and summed in bfloat16 or wider, within the bound.
A program may use at most 64 MiB of HBM per device.

```python
import jax
import jax.numpy as jnp
from jax import lax

FEAT = 256
VECS = 64
ROWS = 512
NPTS = 8192


def block_scale(key, extent, cuts, least, high):
    gain = 1.0
    for dim, shards_of in cuts:
        heights = jax.random.uniform(jax.random.fold_in(jax.random.fold_in(key, 6), dim), (shards_of,), jnp.float32, least / len(cuts), high / len(cuts))
        gain = gain * jnp.repeat(jnp.exp(heights), extent[dim] // shards_of).reshape((-1,) + (1,) * (len(extent) - 1 - dim))
    return gain


def centred(own_key, dims, width, bound, cuts=(), held_as=jnp.bfloat16):
    factor_of = block_scale(own_key, dims, cuts, -0.22, 0.18) if cuts else 1.0
    drawn = jax.random.normal(own_key, dims, jnp.float32) * width * factor_of
    return jnp.minimum(jnp.maximum(drawn, -bound), bound).astype(held_as)


def setup_inputs(seed: int = 0, part: int = 0) -> dict:
    key_list = jax.random.split(jax.random.key(seed), 4)
    part_splits = jax.random.split(jax.random.fold_in(key_list[3], part), 4)
    points = centred(part_splits[0], (NPTS, FEAT), 1.0, 6.0, ((0, 16),))
    left_vec = centred(part_splits[1], (NPTS, VECS), 1.0, 6.0, ((0, 16),))
    right_vec = centred(part_splits[2], (NPTS, VECS), 1.0, 6.0, ((0, 16),))
    return {"points": points, "left_vec": left_vec, "right_vec": right_vec}


def pair_terms(own_x, own_left, far_x, far_right):
    gram = lax.dot_general(own_x, far_x, (((1,), (1,)), ((), ())), preferred_element_type=jnp.float32)
    own_sq = lax.optimization_barrier(jnp.sum(jnp.square(own_x.astype(jnp.float32)), axis=1))
    far_sq = lax.optimization_barrier(jnp.sum(jnp.square(far_x.astype(jnp.float32)), axis=1))
    kernel = jnp.exp(-(own_sq[:, None] + far_sq[None, :] - 2.0 * gram) / FEAT)
    kernel_bf = kernel.astype(jnp.bfloat16)
    inner = lax.dot_general(own_left, far_right, (((1,), (1,)), ((), ())), preferred_element_type=jnp.float32)
    mixed = kernel * inner
    mixed_bf = mixed.astype(jnp.bfloat16)
    near_vu = jnp.dot(kernel_bf, far_right, preferred_element_type=jnp.float32)
    near_grad = jnp.dot(mixed_bf, far_x, preferred_element_type=jnp.float32) - lax.optimization_barrier(jnp.sum(mixed, axis=1))[:, None] * own_x.astype(jnp.float32)
    return (near_vu, near_grad)

def reference(points, left_vec, right_vec):
    far_right = jnp.concatenate([right_vec, left_vec], axis=1)
    scale = 1.0 / jnp.sqrt(jnp.float32(NPTS))

    def block(index):
        start = (index * ROWS).astype(jnp.int32)
        own_x = lax.dynamic_slice_in_dim(points, start, ROWS, 0)
        own_u = lax.dynamic_slice_in_dim(left_vec, start, ROWS, 0)
        own_v = lax.dynamic_slice_in_dim(right_vec, start, ROWS, 0)
        own_left = jnp.concatenate([own_u, own_v], axis=1)
        near_vu, near_grad = pair_terms(own_x, own_left, points, far_right)
        return (near_vu * scale, near_grad * scale)
    block_vu, block_grad = lax.map(block, jnp.arange(NPTS // ROWS, dtype=jnp.int32))
    return (block_vu.reshape(NPTS, 2 * VECS), block_grad.reshape(NPTS, FEAT))
```

```python
import functools
import math

import jax
import jax.numpy as jnp
from jax import lax
from jax.experimental import pallas as pl
from jax.experimental.pallas import tpu as pltpu
from jax.sharding import PartitionSpec as P

MESH = pl.DeviceIdType.MESH
CHUNKS = 2
PARTS = 2
NT = (((1,), (1,)), ((), ()))


def row_squares(block):
    wide = block.astype(jnp.float32)
    return jnp.sum(wide * wide, axis=1, keepdims=True)


def column_squares(block):
    wide = block.astype(jnp.float32)
    square = wide * wide
    high = square.astype(jnp.bfloat16)
    low = (square - high.astype(jnp.float32)).astype(jnp.bfloat16)
    ones = jnp.ones((16, block.shape[1]), jnp.bfloat16)
    total = lax.dot_general(ones, high, NT, preferred_element_type=jnp.float32)
    total += lax.dot_general(ones, low, NT, preferred_element_type=jnp.float32)
    return total[:1]


def pair_block(rows_x, rows_left, rows_sq, cols_x, cols_right, cols_sq):
    slope = 2.0 * math.log2(math.e) / rows_x.shape[1]
    gram = lax.dot_general(rows_x, cols_x, NT, preferred_element_type=jnp.float32)
    inner = lax.dot_general(rows_left, cols_right, NT, preferred_element_type=jnp.float32)
    kernel = jnp.exp2(gram * slope - rows_sq - cols_sq)
    mixed = kernel * inner
    vu = jnp.dot(kernel.astype(jnp.bfloat16), cols_right, preferred_element_type=jnp.float32)
    grad = jnp.dot(mixed.astype(jnp.bfloat16), cols_x, preferred_element_type=jnp.float32)
    sums = mixed[:, :128]
    for at in range(128, mixed.shape[1], 128):
        sums += mixed[:, at : at + 128]
    return vu, grad, sums


def swap_halves(right):
    half = right.shape[1] // 2
    return jnp.concatenate([right[:, half:], right[:, :half]], axis=1)


def paired_kernel(
    depth, points, left, right, out_vu, out_grad,
    blocks, lefts, squares, acc_vu, acc_grad, acc_sum, res_out, res_in,
    recv, send_part, send_mid, send_sib, send_side, send_res, recv_res,
):
    rows, feat = points.shape
    vecs = left.shape[1]
    size = rows // CHUNKS
    group, me = lax.axis_index("groups"), lax.axis_index("blk")
    z, y, c = me // 4, lax.rem(me // 2, 2), lax.rem(me, 2)
    upper = z // 2
    inner = jnp.logical_or(z == 1, z == 2)
    part_z = z + 1 - 2 * lax.rem(z, 2)

    def slot_of(plane, yy, cc):
        return plane * 4 + yy * 2 + cc

    partner = slot_of(part_z, y, c)
    mid = slot_of(3 - z, y, c)
    sib = slot_of(z, y, 1 - c)
    side = slot_of(z, 1 - y, c)
    first = jnp.where(inner, 3 - z, z)
    second = jnp.where(inner, 3 * (1 - upper), part_z)

    def view(slot, chunk):
        return blocks.at[slot, pl.ds(pl.multiple_of(chunk * size, size), size), :]

    def copy(slot, chunk, send, target):
        return pltpu.make_async_remote_copy(
            src_ref=view(slot, chunk),
            dst_ref=view(slot, chunk),
            send_sem=send,
            recv_sem=recv.at[slot * CHUNKS + chunk],
            device_id=(group, target),
            device_id_type=MESH,
        )

    def plane_of(t):
        return jnp.where(t < CHUNKS, first, second)

    def arrived(slot, chunk):
        copy(slot, chunk, send_part.at[0], partner).wait_recv()

    barrier = pltpu.get_barrier_semaphore()
    for other in (partner, sib, side):
        pl.semaphore_signal(barrier, inc=1, device_id=(group, other), device_id_type=MESH)

    @pl.when(inner)
    def _():
        pl.semaphore_signal(barrier, inc=1, device_id=(group, mid), device_id_type=MESH)

    blocks[me, :, :feat] = points[...]
    blocks[me, :, feat:] = jnp.concatenate([right[...], left[...]], axis=1)
    pl.semaphore_wait(barrier, jnp.where(inner, 4, 3))

    for chunk in range(CHUNKS):
        copy(me, chunk, send_part.at[chunk], partner).start()

        @pl.when(inner)
        def _():
            copy(me, chunk, send_mid.at[chunk], mid).start()

    half_log = math.log2(math.e) / feat

    def set_rows(which, slot):
        block = blocks[slot]
        lefts[which] = swap_halves(block[:, feat:])
        squares[which] = jnp.broadcast_to(row_squares(block[:, :feat]) * half_log, (rows, 128))

    set_rows(0, me)
    acc_vu[...] = jnp.zeros_like(acc_vu)
    acc_grad[...] = jnp.zeros_like(acc_grad)
    acc_sum[...] = jnp.zeros_like(acc_sum)

    strip = 256 if rows % 256 == 0 else rows

    def unit(which, row_slot, slot, chunk):
        span = pl.ds(pl.multiple_of(chunk * size, size), size)
        cols_x = blocks[slot, span, :feat]
        cols_right = blocks[slot, span, feat:]
        cols_sq = column_squares(cols_x) * half_log
        for at in range(0, rows, strip):
            here = pl.ds(at, strip)
            sq = squares[which, here, :]
            vu, grad, sums = pair_block(
                blocks[row_slot, here, :feat], lefts[which, here, :],
                jnp.concatenate([sq] * (size // 128), axis=1),
                cols_x, cols_right, cols_sq,
            )
            acc_vu[which, here, :] += vu
            acc_grad[which, here, :] += grad
            acc_sum[which, here, :] += sums

    def result(piece):
        span = rows // PARTS
        at = pl.ds(piece * span, span)
        return pltpu.make_async_remote_copy(
            src_ref=res_out.at[at, :],
            dst_ref=res_in.at[at, :],
            send_sem=send_res.at[piece],
            recv_sem=recv_res.at[piece],
            device_id=(group, partner),
            device_id_type=MESH,
        )

    def step(s, carry):
        fresh = s < 2 * CHUNKS

        @pl.when(fresh)
        def _():
            chunk = lax.rem(s, CHUNKS)
            slot = slot_of(plane_of(s), y, c)

            @pl.when(inner)
            def _():
                arrived(slot, chunk)

            @pl.when(jnp.logical_and(jnp.logical_not(inner), s == CHUNKS))
            def _():
                for piece in range(CHUNKS):
                    arrived(partner, piece)

            copy(slot, chunk, send_side.at[s], side).start()
            copy(slot, chunk, send_sib.at[s], sib).start()

            @pl.when(jnp.logical_and(inner, s < CHUNKS))
            def _():
                arrived(partner, chunk)
                copy(partner, chunk, send_mid.at[CHUNKS + chunk], mid).start()

        @pl.when(s >= 1)
        def _():
            t = s - 1
            chunk = lax.rem(t, CHUNKS)
            slot = slot_of(plane_of(t), 1 - y, c)
            arrived(slot, chunk)
            copy(slot, chunk, send_sib.at[2 * CHUNKS + t], sib).start()
            arrived(slot_of(plane_of(t), 1 - y, 1 - c), chunk)

        @pl.when(fresh)
        def _():
            arrived(slot_of(plane_of(s), y, 1 - c), lax.rem(s, CHUNKS))

        @pl.when(s == CHUNKS)
        def _():
            set_rows(1, partner)

        def job(j, carry):
            kind = j // 2
            back = jnp.logical_or(jnp.logical_or(kind == 1, kind == 3), kind == 5)
            catch = kind < 2
            t = jnp.where(catch, s - CHUNKS, jnp.where(back, s - 1, s))
            low = jnp.where(jnp.logical_or(kind == 2, kind == 3), CHUNKS, 0)
            ok = jnp.logical_and(t >= low, t < 2 * CHUNKS)
            ok = jnp.logical_and(ok, jnp.logical_or(jnp.logical_not(catch), fresh))
            which = jnp.where(kind < 4, 1, 0)

            @pl.when(ok)
            def _():
                yy = jnp.where(back, 1 - y, y)
                cc = jnp.where(lax.rem(j, 2) == 0, c, 1 - c)
                slot = slot_of(plane_of(t), yy, cc)
                unit(which, jnp.where(which == 0, me, partner), slot, lax.rem(t, CHUNKS))

            @pl.when(jnp.logical_and(j == 7, jnp.logical_not(fresh)))
            def _():
                for piece in range(PARTS):
                    span = rows // PARTS
                    at = pl.ds(piece * span, span)
                    total = jnp.sum(acc_sum[1, at, :], axis=1, keepdims=True)
                    x = blocks[partner, at, :feat].astype(jnp.float32)
                    res_out[at, feat:] = acc_vu[1, at, :].astype(jnp.bfloat16)
                    res_out[at, :feat] = (acc_grad[1, at, :] - total * x).astype(jnp.bfloat16)
                    result(piece).start()

            return carry

        return lax.fori_loop(0, 12, job, carry)

    lax.fori_loop(0, 2 * CHUNKS + 1, step, 0)

    scale = 1.0 / math.sqrt(rows * depth)
    for piece in range(PARTS):
        span = rows // PARTS
        at = pl.ds(piece * span, span)
        total = jnp.sum(acc_sum[0, at, :], axis=1, keepdims=True)
        x = blocks[me, at, :feat].astype(jnp.float32)
        grad = acc_grad[0, at, :] - total * x
        result(piece).wait_recv()
        out_vu[at, :] = (acc_vu[0, at, :] + res_in[at, feat:].astype(jnp.float32)) * scale
        out_grad[at, :] = (grad + res_in[at, :feat].astype(jnp.float32)) * scale

    for piece in range(PARTS):
        result(piece).wait_send()
    for chunk in range(CHUNKS):
        copy(me, chunk, send_part.at[chunk], partner).wait_send()
    for t in range(2 * CHUNKS):
        chunk = t % CHUNKS
        plane = first if t < CHUNKS else second
        copy(slot_of(plane, y, c), chunk, send_side.at[t], side).wait_send()
        copy(slot_of(plane, y, c), chunk, send_sib.at[t], sib).wait_send()
        copy(slot_of(plane, 1 - y, c), chunk, send_sib.at[2 * CHUNKS + t], sib).wait_send()

    @pl.when(inner)
    def _():
        for chunk in range(CHUNKS):
            copy(me, chunk, send_mid.at[chunk], mid).wait_send()
            copy(partner, chunk, send_mid.at[CHUNKS + chunk], mid).wait_send()


def paired_device(depth, points, left, right):
    rows, feat = points.shape
    wide = 2 * left.shape[1]
    bf, f32, dma = jnp.bfloat16, jnp.float32, pltpu.SemaphoreType.DMA
    return tuple(
        pl.pallas_call(
            functools.partial(paired_kernel, depth),
            out_shape=(
                jax.ShapeDtypeStruct((rows, wide), f32),
                jax.ShapeDtypeStruct((rows, feat), f32),
            ),
            in_specs=[pl.BlockSpec(memory_space=pltpu.VMEM)] * 3,
            out_specs=[pl.BlockSpec(memory_space=pltpu.VMEM)] * 2,
            scratch_shapes=[
                pltpu.VMEM((depth, rows, feat + wide), bf),
                pltpu.VMEM((2, rows, wide), bf),
                pltpu.VMEM((2, rows, 128), f32),
                pltpu.VMEM((2, rows, wide), f32),
                pltpu.VMEM((2, rows, feat), f32),
                pltpu.VMEM((2, rows, 128), f32),
                pltpu.VMEM((rows, feat + wide), bf),
                pltpu.VMEM((rows, feat + wide), bf),
                dma((depth * CHUNKS,)),
                dma((CHUNKS,)),
                dma((2 * CHUNKS,)),
                dma((4 * CHUNKS,)),
                dma((2 * CHUNKS,)),
                dma((PARTS,)),
                dma((PARTS,)),
            ],
            compiler_params=pltpu.CompilerParams(
                collective_id=0, has_side_effects=True, vmem_limit_bytes=48 * 2**20
            ),
        )(points, left, right)
    )


def gathered_kernel(depth, points, left, right, all_x, all_right, out_vu, out_grad, acc_sum):
    step = pl.program_id(0)
    feat = points.shape[1]
    half_log = math.log2(math.e) / feat
    scale = 1.0 / math.sqrt(points.shape[0] * depth)

    @pl.when(step == 0)
    def _():
        out_vu[...] = jnp.zeros_like(out_vu)
        out_grad[...] = jnp.zeros_like(out_grad)
        acc_sum[...] = jnp.zeros_like(acc_sum)

    own_left = jnp.concatenate([left[...], right[...]], axis=1)
    vu, grad, sums = pair_block(
        points[...], own_left, row_squares(points[...]) * half_log,
        all_x[...], all_right[...], column_squares(all_x[...]) * half_log,
    )
    out_vu[...] += vu
    out_grad[...] += grad
    acc_sum[...] += sums

    @pl.when(step == pl.num_programs(0) - 1)
    def _():
        total = jnp.sum(acc_sum[...], axis=1, keepdims=True)
        out_vu[...] = out_vu[...] * scale
        out_grad[...] = (out_grad[...] - total * points[...].astype(jnp.float32)) * scale


def gathered_device(depth, points, left, right):
    rows, feat = points.shape
    wide = 2 * left.shape[1]
    own_right = jnp.concatenate([right, left], axis=1)
    all_x = lax.all_gather(points, "blk", tiled=True)
    all_right = lax.all_gather(own_right, "blk", tiled=True)
    tile = 256

    def whole(array):
        return pl.BlockSpec(array.shape, lambda i: (0, 0))

    return tuple(
        pl.pallas_call(
            functools.partial(gathered_kernel, depth),
            grid=(rows * depth // tile,),
            out_shape=(
                jax.ShapeDtypeStruct((rows, wide), jnp.float32),
                jax.ShapeDtypeStruct((rows, feat), jnp.float32),
            ),
            in_specs=[
                whole(points), whole(left), whole(right),
                pl.BlockSpec((tile, feat), lambda i: (i, 0)),
                pl.BlockSpec((tile, wide), lambda i: (i, 0)),
            ],
            out_specs=[
                pl.BlockSpec((rows, wide), lambda i: (0, 0)),
                pl.BlockSpec((rows, feat), lambda i: (0, 0)),
            ],
            scratch_shapes=[pltpu.VMEM((rows, 128), jnp.float32)],
            compiler_params=pltpu.CompilerParams(vmem_limit_bytes=32 * 2**20),
        )(points, left, right, all_x, all_right)
    )


def solution(mesh):
    depth = mesh.shape["blk"]
    per_device = paired_device if depth == 16 else gathered_device
    spec = P(("groups", "blk"), None)
    return jax.shard_map(
        functools.partial(per_device, depth),
        mesh=mesh,
        in_specs=(spec, spec, spec),
        out_specs=(spec, spec),
        check_vma=False,
    )
```

```python
import functools
import math

import jax
import jax.numpy as jnp
from jax import lax
from jax.experimental import pallas as pl
from jax.experimental.pallas import tpu as pltpu
from jax.sharding import PartitionSpec as P

MESH = pl.DeviceIdType.MESH
CHUNKS = 4
PARTS = 4
NT = (((1,), (1,)), ((), ()))


def row_squares(block):
    wide = block.astype(jnp.float32)
    return jnp.sum(wide * wide, axis=1, keepdims=True)


def column_squares(block):
    wide = block.astype(jnp.float32)
    square = wide * wide
    high = square.astype(jnp.bfloat16)
    low = (square - high.astype(jnp.float32)).astype(jnp.bfloat16)
    ones = jnp.ones((16, block.shape[1]), jnp.bfloat16)
    total = lax.dot_general(ones, high, NT, preferred_element_type=jnp.float32)
    total += lax.dot_general(ones, low, NT, preferred_element_type=jnp.float32)
    return total[:1]


def pair_block(rows_x, rows_left, rows_sq, cols_x, cols_right, cols_sq):
    slope = 2.0 * math.log2(math.e) / rows_x.shape[1]
    gram = lax.dot_general(rows_x, cols_x, NT, preferred_element_type=jnp.float32)
    inner = lax.dot_general(rows_left, cols_right, NT, preferred_element_type=jnp.float32)
    kernel = jnp.exp2(gram * slope - rows_sq - cols_sq)
    mixed = kernel * inner
    vu = jnp.dot(kernel.astype(jnp.bfloat16), cols_right, preferred_element_type=jnp.float32)
    grad = jnp.dot(mixed.astype(jnp.bfloat16), cols_x, preferred_element_type=jnp.float32)
    sums = mixed[:, :128]
    for at in range(128, mixed.shape[1], 128):
        sums += mixed[:, at : at + 128]
    return vu, grad, sums


def swap_halves(right):
    half = right.shape[1] // 2
    return jnp.concatenate([right[:, half:], right[:, :half]], axis=1)


def paired_kernel(
    depth, points, left, right, out_vu, out_grad,
    blocks, lefts, squares, acc_vu, acc_grad, acc_sum, res_out, res_in,
    recv, send_part, send_mid, send_sib, send_side, send_res, recv_res,
):
    rows, feat = points.shape
    vecs = left.shape[1]
    size = rows // CHUNKS
    group, me = lax.axis_index("groups"), lax.axis_index("blk")
    z, y, c = me // 4, lax.rem(me // 2, 2), lax.rem(me, 2)
    upper = z // 2
    inner = jnp.logical_or(z == 1, z == 2)
    part_z = z + 1 - 2 * lax.rem(z, 2)

    def slot_of(plane, yy, cc):
        return plane * 4 + yy * 2 + cc

    partner = slot_of(part_z, y, c)
    mid = slot_of(3 - z, y, c)
    sib = slot_of(z, y, 1 - c)
    side = slot_of(z, 1 - y, c)
    first = jnp.where(inner, 3 - z, z)
    second = jnp.where(inner, 3 * (1 - upper), part_z)

    def view(slot, chunk):
        return blocks.at[slot, pl.ds(pl.multiple_of(chunk * size, size), size), :]

    def copy(slot, chunk, send, target):
        return pltpu.make_async_remote_copy(
            src_ref=view(slot, chunk),
            dst_ref=view(slot, chunk),
            send_sem=send,
            recv_sem=recv.at[slot * CHUNKS + chunk],
            device_id=(group, target),
            device_id_type=MESH,
        )

    def arrived(slot, chunk):
        copy(slot, chunk, send_part.at[0], partner).wait_recv()

    barrier = pltpu.get_barrier_semaphore()
    for other in (partner, sib, side):
        pl.semaphore_signal(barrier, inc=1, device_id=(group, other), device_id_type=MESH)

    @pl.when(inner)
    def _():
        pl.semaphore_signal(barrier, inc=1, device_id=(group, mid), device_id_type=MESH)

    blocks[me, :, :feat] = points[...]
    blocks[me, :, feat:] = jnp.concatenate([right[...], left[...]], axis=1)
    pl.semaphore_wait(barrier, jnp.where(inner, 4, 3))

    for chunk in range(CHUNKS):
        copy(me, chunk, send_part.at[chunk], partner).start()

        @pl.when(inner)
        def _():
            copy(me, chunk, send_mid.at[chunk], mid).start()

    half_log = math.log2(math.e) / feat

    def set_rows(which, slot):
        block = blocks[slot]
        lefts[which] = swap_halves(block[:, feat:])
        squares[which] = jnp.broadcast_to(row_squares(block[:, :feat]) * half_log, (rows, 128))

    set_rows(0, me)
    acc_vu[...] = jnp.zeros_like(acc_vu)
    acc_grad[...] = jnp.zeros_like(acc_grad)
    acc_sum[...] = jnp.zeros_like(acc_sum)

    strip = rows

    def unit(which, order, yy, begin, length):
        first_slot = slot_of(first if order == 0 else second, yy, 0)
        span = pl.ds(begin, length)
        cols_x = blocks[pl.ds(first_slot, 2), span, :feat].reshape(2 * length, feat)
        cols_right = blocks[pl.ds(first_slot, 2), span, feat:].reshape(2 * length, -1)
        cols_sq = column_squares(cols_x) * half_log
        row_slot = partner if which else me
        for at in range(0, rows, strip):
            here = pl.ds(at, strip)
            sq = squares[which, here, :]
            vu, grad, sums = pair_block(
                blocks[row_slot, here, :feat], lefts[which, here, :],
                jnp.concatenate([sq] * (2 * length // 128), axis=1),
                cols_x, cols_right, cols_sq,
            )
            acc_vu[which, here, :] += vu
            acc_grad[which, here, :] += grad
            acc_sum[which, here, :] += sums

    def result(piece):
        span = rows // PARTS
        at = pl.ds(piece * span, span)
        return pltpu.make_async_remote_copy(
            src_ref=res_out.at[at, :],
            dst_ref=res_in.at[at, :],
            send_sem=send_res.at[piece],
            recv_sem=recv_res.at[piece],
            device_id=(group, partner),
            device_id_type=MESH,
        )

    def planes(t):
        return first if t < CHUNKS else second

    def from_line(t):
        chunk = t % CHUNKS
        slot = slot_of(planes(t), y, c)

        @pl.when(inner)
        def _():
            arrived(slot, chunk)

        copy(slot, chunk, send_side.at[t], side).start()
        copy(slot, chunk, send_sib.at[t], sib).start()
        if t < CHUNKS:
            arrived(partner, chunk)

            @pl.when(inner)
            def _():
                copy(partner, chunk, send_mid.at[CHUNKS + chunk], mid).start()

    def from_side(t):
        chunk = t % CHUNKS
        slot = slot_of(planes(t), 1 - y, c)
        arrived(slot, chunk)
        copy(slot, chunk, send_sib.at[2 * CHUNKS + t], sib).start()

    def sib_line(t):
        arrived(slot_of(planes(t), y, 1 - c), t % CHUNKS)

    def sib_side(t):
        arrived(slot_of(planes(t), 1 - y, 1 - c), t % CHUNKS)

    half = rows // 2
    for t in range(2 * CHUNKS):
        from_line(t)
        if t >= 1:
            from_side(t - 1)
        if t == 2:
            for u in (0, 1):
                sib_line(u)
            unit(0, 0, y, 0, half)
        elif t == 3:
            for u in (0, 1):
                sib_side(u)
            unit(0, 0, 1 - y, 0, half)
        elif t == 4:
            set_rows(1, partner)
            for u in (2, 3):
                sib_line(u)
            unit(1, 0, y, 0, rows)
        elif t == 5:
            for u in (2, 3):
                sib_side(u)
            unit(1, 0, 1 - y, 0, rows)
        elif t == 6:
            for u in (4, 5):
                sib_line(u)
            unit(1, 1, y, 0, half)
            unit(0, 0, y, half, half)
        elif t == 7:
            for u in (4, 5):
                sib_side(u)
            unit(1, 1, 1 - y, 0, half)
            for u in (6, 7):
                sib_line(u)
            unit(1, 1, y, half, half)
    from_side(2 * CHUNKS - 1)
    for u in (6, 7):
        sib_side(u)
    unit(1, 1, 1 - y, half, half)

    for piece in range(PARTS):
        span = rows // PARTS
        at = pl.ds(piece * span, span)
        total = jnp.sum(acc_sum[1, at, :], axis=1, keepdims=True)
        x = blocks[partner, at, :feat].astype(jnp.float32)
        res_out[at, feat:] = acc_vu[1, at, :].astype(jnp.bfloat16)
        res_out[at, :feat] = (acc_grad[1, at, :] - total * x).astype(jnp.bfloat16)
        result(piece).start()

    unit(0, 0, 1 - y, half, half)
    unit(0, 1, y, 0, rows)
    unit(0, 1, 1 - y, 0, rows)

    scale = 1.0 / math.sqrt(rows * depth)
    for piece in range(PARTS):
        span = rows // PARTS
        at = pl.ds(piece * span, span)
        total = jnp.sum(acc_sum[0, at, :], axis=1, keepdims=True)
        x = blocks[me, at, :feat].astype(jnp.float32)
        grad = acc_grad[0, at, :] - total * x
        result(piece).wait_recv()
        out_vu[at, :] = (acc_vu[0, at, :] + res_in[at, feat:].astype(jnp.float32)) * scale
        out_grad[at, :] = (grad + res_in[at, :feat].astype(jnp.float32)) * scale

    for piece in range(PARTS):
        result(piece).wait_send()
    for chunk in range(CHUNKS):
        copy(me, chunk, send_part.at[chunk], partner).wait_send()
    for t in range(2 * CHUNKS):
        chunk = t % CHUNKS
        plane = first if t < CHUNKS else second
        copy(slot_of(plane, y, c), chunk, send_side.at[t], side).wait_send()
        copy(slot_of(plane, y, c), chunk, send_sib.at[t], sib).wait_send()
        copy(slot_of(plane, 1 - y, c), chunk, send_sib.at[2 * CHUNKS + t], sib).wait_send()

    @pl.when(inner)
    def _():
        for chunk in range(CHUNKS):
            copy(me, chunk, send_mid.at[chunk], mid).wait_send()
            copy(partner, chunk, send_mid.at[CHUNKS + chunk], mid).wait_send()


def paired_device(depth, points, left, right):
    rows, feat = points.shape
    wide = 2 * left.shape[1]
    bf, f32, dma = jnp.bfloat16, jnp.float32, pltpu.SemaphoreType.DMA
    return tuple(
        pl.pallas_call(
            functools.partial(paired_kernel, depth),
            out_shape=(
                jax.ShapeDtypeStruct((rows, wide), f32),
                jax.ShapeDtypeStruct((rows, feat), f32),
            ),
            in_specs=[pl.BlockSpec(memory_space=pltpu.VMEM)] * 3,
            out_specs=[pl.BlockSpec(memory_space=pltpu.VMEM)] * 2,
            scratch_shapes=[
                pltpu.VMEM((depth, rows, feat + wide), bf),
                pltpu.VMEM((2, rows, wide), bf),
                pltpu.VMEM((2, rows, 128), f32),
                pltpu.VMEM((2, rows, wide), f32),
                pltpu.VMEM((2, rows, feat), f32),
                pltpu.VMEM((2, rows, 128), f32),
                pltpu.VMEM((rows, feat + wide), bf),
                pltpu.VMEM((rows, feat + wide), bf),
                dma((depth * CHUNKS,)),
                dma((CHUNKS,)),
                dma((2 * CHUNKS,)),
                dma((4 * CHUNKS,)),
                dma((2 * CHUNKS,)),
                dma((PARTS,)),
                dma((PARTS,)),
            ],
            compiler_params=pltpu.CompilerParams(
                collective_id=0, has_side_effects=True, vmem_limit_bytes=48 * 2**20
            ),
        )(points, left, right)
    )


def gathered_kernel(depth, points, left, right, all_x, all_right, out_vu, out_grad, acc_sum):
    step = pl.program_id(0)
    feat = points.shape[1]
    half_log = math.log2(math.e) / feat
    scale = 1.0 / math.sqrt(points.shape[0] * depth)

    @pl.when(step == 0)
    def _():
        out_vu[...] = jnp.zeros_like(out_vu)
        out_grad[...] = jnp.zeros_like(out_grad)
        acc_sum[...] = jnp.zeros_like(acc_sum)

    own_left = jnp.concatenate([left[...], right[...]], axis=1)
    vu, grad, sums = pair_block(
        points[...], own_left, row_squares(points[...]) * half_log,
        all_x[...], all_right[...], column_squares(all_x[...]) * half_log,
    )
    out_vu[...] += vu
    out_grad[...] += grad
    acc_sum[...] += sums

    @pl.when(step == pl.num_programs(0) - 1)
    def _():
        total = jnp.sum(acc_sum[...], axis=1, keepdims=True)
        out_vu[...] = out_vu[...] * scale
        out_grad[...] = (out_grad[...] - total * points[...].astype(jnp.float32)) * scale


def gathered_device(depth, points, left, right):
    rows, feat = points.shape
    wide = 2 * left.shape[1]
    own_right = jnp.concatenate([right, left], axis=1)
    all_x = lax.all_gather(points, "blk", tiled=True)
    all_right = lax.all_gather(own_right, "blk", tiled=True)
    tile = 256

    def whole(array):
        return pl.BlockSpec(array.shape, lambda i: (0, 0))

    return tuple(
        pl.pallas_call(
            functools.partial(gathered_kernel, depth),
            grid=(rows * depth // tile,),
            out_shape=(
                jax.ShapeDtypeStruct((rows, wide), jnp.float32),
                jax.ShapeDtypeStruct((rows, feat), jnp.float32),
            ),
            in_specs=[
                whole(points), whole(left), whole(right),
                pl.BlockSpec((tile, feat), lambda i: (i, 0)),
                pl.BlockSpec((tile, wide), lambda i: (i, 0)),
            ],
            out_specs=[
                pl.BlockSpec((rows, wide), lambda i: (0, 0)),
                pl.BlockSpec((rows, feat), lambda i: (0, 0)),
            ],
            scratch_shapes=[pltpu.VMEM((rows, 128), jnp.float32)],
            compiler_params=pltpu.CompilerParams(vmem_limit_bytes=32 * 2**20),
        )(points, left, right, all_x, all_right)
    )


def solution(mesh):
    depth = mesh.shape["blk"]
    per_device = paired_device if depth == 16 else gathered_device
    spec = P(("groups", "blk"), None)
    return jax.shard_map(
        functools.partial(per_device, depth),
        mesh=mesh,
        in_specs=(spec, spec, spec),
        out_specs=(spec, spec),
        check_vma=False,
    )
```

```python
import functools
import math

import jax
import jax.numpy as jnp
from jax import lax
from jax.experimental import pallas as pl
from jax.experimental.pallas import tpu as pltpu
from jax.sharding import PartitionSpec as P

MESH = pl.DeviceIdType.MESH
CHUNKS = 4
WINDOW = 3
SKEW = 2
PARTS = 4
NT = (((1,), (1,)), ((), ()))


def row_squares(block):
    wide = block.astype(jnp.float32)
    return jnp.sum(wide * wide, axis=1, keepdims=True)


def column_squares(block):
    wide = block.astype(jnp.float32)
    square = wide * wide
    high = square.astype(jnp.bfloat16)
    low = (square - high.astype(jnp.float32)).astype(jnp.bfloat16)
    ones = jnp.ones((16, block.shape[1]), jnp.bfloat16)
    total = lax.dot_general(ones, high, NT, preferred_element_type=jnp.float32)
    total += lax.dot_general(ones, low, NT, preferred_element_type=jnp.float32)
    return total[:1]


def pair_block(rows_x, rows_left, rows_sq, cols_x, cols_right, cols_sq):
    slope = 2.0 * math.log2(math.e) / rows_x.shape[1]
    gram = lax.dot_general(rows_x, cols_x, NT, preferred_element_type=jnp.float32)
    inner = lax.dot_general(rows_left, cols_right, NT, preferred_element_type=jnp.float32)
    kernel = jnp.exp2(gram * slope - rows_sq - cols_sq)
    mixed = kernel * inner
    vu = jnp.dot(kernel.astype(jnp.bfloat16), cols_right, preferred_element_type=jnp.float32)
    grad = jnp.dot(mixed.astype(jnp.bfloat16), cols_x, preferred_element_type=jnp.float32)
    sums = mixed[:, :128]
    for at in range(128, mixed.shape[1], 128):
        sums += mixed[:, at : at + 128]
    return vu, grad, sums


def swap_halves(right):
    half = right.shape[1] // 2
    return jnp.concatenate([right[:, half:], right[:, :half]], axis=1)


def paired_kernel(
    depth, points, left, right, out_vu, out_grad,
    blocks, lefts, squares, acc_vu, acc_grad, acc_sum, res_out, res_in,
    recv, send_part, send_mid, send_sib, send_side, send_res, recv_res,
):
    rows, feat = points.shape
    vecs = left.shape[1]
    size = rows // CHUNKS
    group, me = lax.axis_index("groups"), lax.axis_index("blk")
    z, y, c = me // 4, lax.rem(me // 2, 2), lax.rem(me, 2)
    upper = z // 2
    inner = jnp.logical_or(z == 1, z == 2)
    part_z = z + 1 - 2 * lax.rem(z, 2)

    def slot_of(plane, yy, cc):
        return plane * 4 + yy * 2 + cc

    partner = slot_of(part_z, y, c)
    mid = slot_of(3 - z, y, c)
    sib = slot_of(z, y, 1 - c)
    side = slot_of(z, 1 - y, c)
    first = jnp.where(inner, 3 - z, z)
    second = jnp.where(inner, 3 * (1 - upper), part_z)

    def view(slot, chunk):
        return blocks.at[slot, pl.ds(pl.multiple_of(chunk * size, size), size), :]

    def copy(slot, chunk, send, target):
        return pltpu.make_async_remote_copy(
            src_ref=view(slot, chunk),
            dst_ref=view(slot, chunk),
            send_sem=send,
            recv_sem=recv.at[slot * CHUNKS + chunk],
            device_id=(group, target),
            device_id_type=MESH,
        )

    def arrived(slot, chunk):
        copy(slot, chunk, send_part.at[0], partner).wait_recv()

    barrier = pltpu.get_barrier_semaphore()
    for other in (partner, sib, side):
        pl.semaphore_signal(barrier, inc=1, device_id=(group, other), device_id_type=MESH)

    @pl.when(inner)
    def _():
        pl.semaphore_signal(barrier, inc=1, device_id=(group, mid), device_id_type=MESH)

    blocks[me, :, :feat] = points[...]
    blocks[me, :, feat:] = jnp.concatenate([right[...], left[...]], axis=1)
    pl.semaphore_wait(barrier, jnp.where(inner, 4, 3))

    def to_mid(t):
        return copy(me if t < CHUNKS else partner, t % CHUNKS, send_mid.at[t], mid)

    for chunk in range(WINDOW):
        copy(me, chunk, send_part.at[chunk], partner).start()

        @pl.when(inner)
        def _():
            to_mid(chunk).start()

    half_log = math.log2(math.e) / feat

    def set_rows(which, slot):
        block = blocks[slot]
        lefts[which] = swap_halves(block[:, feat:])
        squares[which] = jnp.broadcast_to(row_squares(block[:, :feat]) * half_log, (rows, 128))

    set_rows(0, me)
    acc_vu[...] = jnp.zeros_like(acc_vu)
    acc_grad[...] = jnp.zeros_like(acc_grad)
    acc_sum[...] = jnp.zeros_like(acc_sum)

    strip = rows

    def unit(which, order, yy, begin, length):
        first_slot = slot_of(first if order == 0 else second, yy, 0)
        span = pl.ds(begin, length)
        cols_x = blocks[pl.ds(first_slot, 2), span, :feat].reshape(2 * length, feat)
        cols_right = blocks[pl.ds(first_slot, 2), span, feat:].reshape(2 * length, -1)
        cols_sq = column_squares(cols_x) * half_log
        row_slot = partner if which else me
        for at in range(0, rows, strip):
            here = pl.ds(at, strip)
            sq = squares[which, here, :]
            vu, grad, sums = pair_block(
                blocks[row_slot, here, :feat], lefts[which, here, :],
                jnp.concatenate([sq] * (2 * length // 128), axis=1),
                cols_x, cols_right, cols_sq,
            )
            acc_vu[which, here, :] += vu
            acc_grad[which, here, :] += grad
            acc_sum[which, here, :] += sums

    def result(piece):
        span = rows // PARTS
        at = pl.ds(piece * span, span)
        return pltpu.make_async_remote_copy(
            src_ref=res_out.at[at, :],
            dst_ref=res_in.at[at, :],
            send_sem=send_res.at[piece],
            recv_sem=recv_res.at[piece],
            device_id=(group, partner),
            device_id_type=MESH,
        )

    def planes(t):
        return first if t < CHUNKS else second

    def from_line(t):
        chunk = t % CHUNKS
        slot = slot_of(planes(t), y, c)

        @pl.when(inner)
        def _():
            arrived(slot, chunk)

        copy(slot, chunk, send_side.at[t], side).start()
        copy(slot, chunk, send_sib.at[t], sib).start()
        if t < CHUNKS:
            arrived(partner, chunk)
            if chunk + WINDOW < CHUNKS:
                copy(me, chunk + WINDOW, send_part.at[chunk + WINDOW], partner).start()
        if t + WINDOW < 2 * CHUNKS:

            @pl.when(inner)
            def _():
                to_mid(t + WINDOW).start()

    def from_side(t):
        chunk = t % CHUNKS
        slot = slot_of(planes(t), 1 - y, c)
        arrived(slot, chunk)
        copy(slot, chunk, send_sib.at[2 * CHUNKS + t], sib).start()

    def sib_line(t):
        arrived(slot_of(planes(t), y, 1 - c), t % CHUNKS)

    def sib_side(t):
        arrived(slot_of(planes(t), 1 - y, 1 - c), t % CHUNKS)

    half = rows // 2
    quarter = CHUNKS // 2

    def line_ready(piece):
        for u in range(piece * quarter, (piece + 1) * quarter):
            sib_line(u)

    def side_ready(piece):
        for u in range(piece * quarter, (piece + 1) * quarter):
            sib_side(u)

    for t in range(2 * CHUNKS):
        from_line(t)
        if t >= SKEW:
            from_side(t - SKEW)
        if t == quarter:
            line_ready(0)
            unit(0, 0, y, 0, half)
        elif t == quarter + 1:
            side_ready(0)
            unit(0, 0, 1 - y, 0, half)
        elif t == 2 * quarter:
            set_rows(1, partner)
            line_ready(1)
            unit(1, 0, y, 0, rows)
        elif t == 2 * quarter + 1:
            unit(1, 0, 1 - y, 0, half)
        elif t == 2 * quarter + 2:
            line_ready(2)
            unit(1, 1, y, 0, half)
        elif t == 2 * quarter + 3:
            side_ready(1)
            unit(1, 0, 1 - y, half, half)
    from_side(2 * CHUNKS - 2)
    line_ready(3)
    unit(1, 1, y, half, half)
    side_ready(2)
    unit(1, 1, 1 - y, 0, half)
    from_side(2 * CHUNKS - 1)
    side_ready(3)
    unit(1, 1, 1 - y, half, half)

    for piece in range(PARTS):
        span = rows // PARTS
        at = pl.ds(piece * span, span)
        total = jnp.sum(acc_sum[1, at, :], axis=1, keepdims=True)
        x = blocks[partner, at, :feat].astype(jnp.float32)
        res_out[at, feat:] = acc_vu[1, at, :].astype(jnp.bfloat16)
        res_out[at, :feat] = (acc_grad[1, at, :] - total * x).astype(jnp.bfloat16)
        result(piece).start()

    unit(0, 0, y, half, half)
    unit(0, 0, 1 - y, half, half)
    unit(0, 1, y, 0, rows)
    unit(0, 1, 1 - y, 0, rows)

    scale = 1.0 / math.sqrt(rows * depth)
    for piece in range(PARTS):
        span = rows // PARTS
        at = pl.ds(piece * span, span)
        total = jnp.sum(acc_sum[0, at, :], axis=1, keepdims=True)
        x = blocks[me, at, :feat].astype(jnp.float32)
        grad = acc_grad[0, at, :] - total * x
        result(piece).wait_recv()
        out_vu[at, :] = (acc_vu[0, at, :] + res_in[at, feat:].astype(jnp.float32)) * scale
        out_grad[at, :] = (grad + res_in[at, :feat].astype(jnp.float32)) * scale

    for piece in range(PARTS):
        result(piece).wait_send()
    for chunk in range(CHUNKS):
        copy(me, chunk, send_part.at[chunk], partner).wait_send()
    for t in range(2 * CHUNKS):
        chunk = t % CHUNKS
        plane = first if t < CHUNKS else second
        copy(slot_of(plane, y, c), chunk, send_side.at[t], side).wait_send()
        copy(slot_of(plane, y, c), chunk, send_sib.at[t], sib).wait_send()
        copy(slot_of(plane, 1 - y, c), chunk, send_sib.at[2 * CHUNKS + t], sib).wait_send()

    @pl.when(inner)
    def _():
        for chunk in range(CHUNKS):
            to_mid(chunk).wait_send()
            to_mid(CHUNKS + chunk).wait_send()


def paired_device(depth, points, left, right):
    rows, feat = points.shape
    wide = 2 * left.shape[1]
    bf, f32, dma = jnp.bfloat16, jnp.float32, pltpu.SemaphoreType.DMA
    return tuple(
        pl.pallas_call(
            functools.partial(paired_kernel, depth),
            out_shape=(
                jax.ShapeDtypeStruct((rows, wide), f32),
                jax.ShapeDtypeStruct((rows, feat), f32),
            ),
            in_specs=[pl.BlockSpec(memory_space=pltpu.VMEM)] * 3,
            out_specs=[pl.BlockSpec(memory_space=pltpu.VMEM)] * 2,
            scratch_shapes=[
                pltpu.VMEM((depth, rows, feat + wide), bf),
                pltpu.VMEM((2, rows, wide), bf),
                pltpu.VMEM((2, rows, 128), f32),
                pltpu.VMEM((2, rows, wide), f32),
                pltpu.VMEM((2, rows, feat), f32),
                pltpu.VMEM((2, rows, 128), f32),
                pltpu.VMEM((rows, feat + wide), bf),
                pltpu.VMEM((rows, feat + wide), bf),
                dma((depth * CHUNKS,)),
                dma((CHUNKS,)),
                dma((2 * CHUNKS,)),
                dma((4 * CHUNKS,)),
                dma((2 * CHUNKS,)),
                dma((PARTS,)),
                dma((PARTS,)),
            ],
            compiler_params=pltpu.CompilerParams(
                collective_id=0, has_side_effects=True, vmem_limit_bytes=48 * 2**20
            ),
        )(points, left, right)
    )


def gathered_kernel(depth, points, left, right, all_x, all_right, out_vu, out_grad, acc_sum):
    step = pl.program_id(0)
    feat = points.shape[1]
    half_log = math.log2(math.e) / feat
    scale = 1.0 / math.sqrt(points.shape[0] * depth)

    @pl.when(step == 0)
    def _():
        out_vu[...] = jnp.zeros_like(out_vu)
        out_grad[...] = jnp.zeros_like(out_grad)
        acc_sum[...] = jnp.zeros_like(acc_sum)

    own_left = jnp.concatenate([left[...], right[...]], axis=1)
    vu, grad, sums = pair_block(
        points[...], own_left, row_squares(points[...]) * half_log,
        all_x[...], all_right[...], column_squares(all_x[...]) * half_log,
    )
    out_vu[...] += vu
    out_grad[...] += grad
    acc_sum[...] += sums

    @pl.when(step == pl.num_programs(0) - 1)
    def _():
        total = jnp.sum(acc_sum[...], axis=1, keepdims=True)
        out_vu[...] = out_vu[...] * scale
        out_grad[...] = (out_grad[...] - total * points[...].astype(jnp.float32)) * scale


def gathered_device(depth, points, left, right):
    rows, feat = points.shape
    wide = 2 * left.shape[1]
    own_right = jnp.concatenate([right, left], axis=1)
    all_x = lax.all_gather(points, "blk", tiled=True)
    all_right = lax.all_gather(own_right, "blk", tiled=True)
    tile = 256

    def whole(array):
        return pl.BlockSpec(array.shape, lambda i: (0, 0))

    return tuple(
        pl.pallas_call(
            functools.partial(gathered_kernel, depth),
            grid=(rows * depth // tile,),
            out_shape=(
                jax.ShapeDtypeStruct((rows, wide), jnp.float32),
                jax.ShapeDtypeStruct((rows, feat), jnp.float32),
            ),
            in_specs=[
                whole(points), whole(left), whole(right),
                pl.BlockSpec((tile, feat), lambda i: (i, 0)),
                pl.BlockSpec((tile, wide), lambda i: (i, 0)),
            ],
            out_specs=[
                pl.BlockSpec((rows, wide), lambda i: (0, 0)),
                pl.BlockSpec((rows, feat), lambda i: (0, 0)),
            ],
            scratch_shapes=[pltpu.VMEM((rows, 128), jnp.float32)],
            compiler_params=pltpu.CompilerParams(vmem_limit_bytes=32 * 2**20),
        )(points, left, right, all_x, all_right)
    )


def solution(mesh):
    depth = mesh.shape["blk"]
    per_device = paired_device if depth == 16 else gathered_device
    spec = P(("groups", "blk"), None)
    return jax.shard_map(
        functools.partial(per_device, depth),
        mesh=mesh,
        in_specs=(spec, spec, spec),
        out_specs=(spec, spec),
        check_vma=False,
    )
```

```python
import functools
import math

import jax
import jax.numpy as jnp
from jax import lax
from jax.experimental import pallas as pl
from jax.experimental.pallas import tpu as pltpu
from jax.sharding import PartitionSpec as P

MESH = pl.DeviceIdType.MESH
CHUNKS = 4
WINDOW = 4
SKEW = 2
PARTS = 4
NT = (((1,), (1,)), ((), ()))


def row_squares(block):
    wide = block.astype(jnp.float32)
    return jnp.sum(wide * wide, axis=1, keepdims=True)


def column_squares(block):
    wide = block.astype(jnp.float32)
    square = wide * wide
    high = square.astype(jnp.bfloat16)
    low = (square - high.astype(jnp.float32)).astype(jnp.bfloat16)
    ones = jnp.ones((16, block.shape[1]), jnp.bfloat16)
    total = lax.dot_general(ones, high, NT, preferred_element_type=jnp.float32)
    total += lax.dot_general(ones, low, NT, preferred_element_type=jnp.float32)
    return total[:1]


def pair_block(rows_x, rows_left, rows_sq, cols_x, cols_right, cols_sq):
    slope = 2.0 * math.log2(math.e) / rows_x.shape[1]
    gram = lax.dot_general(rows_x, cols_x, NT, preferred_element_type=jnp.float32)
    inner = lax.dot_general(rows_left, cols_right, NT, preferred_element_type=jnp.float32)
    kernel = jnp.exp2(gram * slope - rows_sq - cols_sq)
    mixed = kernel * inner
    vu = jnp.dot(kernel.astype(jnp.bfloat16), cols_right, preferred_element_type=jnp.float32)
    grad = jnp.dot(mixed.astype(jnp.bfloat16), cols_x, preferred_element_type=jnp.float32)
    sums = mixed[:, :128]
    for at in range(128, mixed.shape[1], 128):
        sums += mixed[:, at : at + 128]
    return vu, grad, sums


def swap_halves(right):
    half = right.shape[1] // 2
    return jnp.concatenate([right[:, half:], right[:, :half]], axis=1)


def paired_kernel(
    depth, points, left, right, out_vu, out_grad,
    blocks, lefts, squares, acc_vu, acc_grad, acc_sum, res_out, res_in,
    recv, send_part, send_mid, send_sib, send_side, send_res, recv_res,
):
    rows, feat = points.shape
    vecs = left.shape[1]
    size = rows // CHUNKS
    group, me = lax.axis_index("groups"), lax.axis_index("blk")
    z, y, c = me // 4, lax.rem(me // 2, 2), lax.rem(me, 2)
    upper = z // 2
    inner = jnp.logical_or(z == 1, z == 2)
    part_z = z + 1 - 2 * lax.rem(z, 2)

    def slot_of(plane, yy, cc):
        return plane * 4 + yy * 2 + cc

    partner = slot_of(part_z, y, c)
    mid = slot_of(3 - z, y, c)
    sib = slot_of(z, y, 1 - c)
    side = slot_of(z, 1 - y, c)
    first = jnp.where(inner, 3 - z, z)
    second = jnp.where(inner, 3 * (1 - upper), part_z)

    def view(slot, chunk):
        return blocks.at[slot, pl.ds(pl.multiple_of(chunk * size, size), size), :]

    def copy(slot, chunk, send, target):
        return pltpu.make_async_remote_copy(
            src_ref=view(slot, chunk),
            dst_ref=view(slot, chunk),
            send_sem=send,
            recv_sem=recv.at[slot * CHUNKS + chunk],
            device_id=(group, target),
            device_id_type=MESH,
        )

    def arrived(slot, chunk):
        copy(slot, chunk, send_part.at[0], partner).wait_recv()

    barrier = pltpu.get_barrier_semaphore()
    for other in (partner, sib, side):
        pl.semaphore_signal(barrier, inc=1, device_id=(group, other), device_id_type=MESH)

    @pl.when(inner)
    def _():
        pl.semaphore_signal(barrier, inc=1, device_id=(group, mid), device_id_type=MESH)

    blocks[me, :, :feat] = points[...]
    blocks[me, :, feat:] = jnp.concatenate([right[...], left[...]], axis=1)
    pl.semaphore_wait(barrier, jnp.where(inner, 4, 3))

    def to_mid(t):
        return copy(me if t < CHUNKS else partner, t % CHUNKS, send_mid.at[t], mid)

    for chunk in range(WINDOW):
        copy(me, chunk, send_part.at[chunk], partner).start()

        @pl.when(inner)
        def _():
            to_mid(chunk).start()

    half_log = math.log2(math.e) / feat

    def set_rows(which, slot):
        block = blocks[slot]
        lefts[which] = swap_halves(block[:, feat:])
        squares[which] = jnp.broadcast_to(row_squares(block[:, :feat]) * half_log, (rows, 128))

    set_rows(0, me)
    acc_vu[...] = jnp.zeros_like(acc_vu)
    acc_grad[...] = jnp.zeros_like(acc_grad)
    acc_sum[...] = jnp.zeros_like(acc_sum)

    def unit(which, order, yy, begin, length, pieces=((0, rows),)):
        first_slot = slot_of(first if order == 0 else second, yy, 0)
        span = pl.ds(begin, length)
        cols_x = blocks[pl.ds(first_slot, 2), span, :feat].reshape(2 * length, feat)
        cols_right = blocks[pl.ds(first_slot, 2), span, feat:].reshape(2 * length, -1)
        cols_sq = column_squares(cols_x) * half_log
        row_slot = partner if which else me
        for at, strip in pieces:
            here = pl.ds(at, strip)
            sq = squares[which, here, :]
            vu, grad, sums = pair_block(
                blocks[row_slot, here, :feat], lefts[which, here, :],
                jnp.concatenate([sq] * (2 * length // 128), axis=1),
                cols_x, cols_right, cols_sq,
            )
            acc_vu[which, here, :] += vu
            acc_grad[which, here, :] += grad
            acc_sum[which, here, :] += sums

    def result(piece):
        span = rows // PARTS
        at = pl.ds(piece * span, span)
        return pltpu.make_async_remote_copy(
            src_ref=res_out.at[at, :],
            dst_ref=res_in.at[at, :],
            send_sem=send_res.at[piece],
            recv_sem=recv_res.at[piece],
            device_id=(group, partner),
            device_id_type=MESH,
        )

    def planes(t):
        return first if t < CHUNKS else second

    def from_line(t):
        chunk = t % CHUNKS
        slot = slot_of(planes(t), y, c)

        @pl.when(inner)
        def _():
            arrived(slot, chunk)

        copy(slot, chunk, send_side.at[t], side).start()
        copy(slot, chunk, send_sib.at[t], sib).start()
        if t < CHUNKS:
            arrived(partner, chunk)
            if chunk + WINDOW < CHUNKS:
                copy(me, chunk + WINDOW, send_part.at[chunk + WINDOW], partner).start()
        if t + WINDOW < 2 * CHUNKS:

            @pl.when(inner)
            def _():
                to_mid(t + WINDOW).start()

    def from_side(t):
        chunk = t % CHUNKS
        slot = slot_of(planes(t), 1 - y, c)
        arrived(slot, chunk)
        copy(slot, chunk, send_sib.at[2 * CHUNKS + t], sib).start()

    def sib_line(t):
        arrived(slot_of(planes(t), y, 1 - c), t % CHUNKS)

    def sib_side(t):
        arrived(slot_of(planes(t), 1 - y, 1 - c), t % CHUNKS)

    half = rows // 2
    quarter = CHUNKS // 2

    def line_ready(piece):
        for u in range(piece * quarter, (piece + 1) * quarter):
            sib_line(u)

    def side_ready(piece):
        for u in range(piece * quarter, (piece + 1) * quarter):
            sib_side(u)

    for t in range(2 * CHUNKS):
        from_line(t)
        if t >= SKEW:
            from_side(t - SKEW)
        if t == quarter:
            line_ready(0)
            unit(0, 0, y, 0, half)
        elif t == quarter + 1:
            side_ready(0)
            unit(0, 0, 1 - y, 0, half)
        elif t == 2 * quarter:
            set_rows(1, partner)
            line_ready(1)
            unit(1, 0, y, 0, rows)
        elif t == 2 * quarter + 1:
            unit(1, 0, 1 - y, 0, half)
        elif t == 2 * quarter + 2:
            line_ready(2)
            unit(1, 1, y, 0, half)
        elif t == 2 * quarter + 3:
            side_ready(1)
            unit(1, 0, 1 - y, half, half)
    from_side(2 * CHUNKS - 2)
    line_ready(3)
    unit(1, 1, y, half, half)
    side_ready(2)
    unit(1, 1, 1 - y, 0, half)
    from_side(2 * CHUNKS - 1)
    side_ready(3)
    span = rows // PARTS
    for piece in range(PARTS):
        unit(1, 1, 1 - y, half, half, ((piece * span, span),))
        at = pl.ds(piece * span, span)
        total = jnp.sum(acc_sum[1, at, :], axis=1, keepdims=True)
        x = blocks[partner, at, :feat].astype(jnp.float32)
        res_out[at, feat:] = acc_vu[1, at, :].astype(jnp.bfloat16)
        res_out[at, :feat] = (acc_grad[1, at, :] - total * x).astype(jnp.bfloat16)
        result(piece).start()

    unit(0, 0, y, half, half)
    unit(0, 0, 1 - y, half, half)
    unit(0, 1, y, 0, rows)
    unit(0, 1, 1 - y, 0, rows)

    scale = 1.0 / math.sqrt(rows * depth)
    for piece in range(PARTS):
        span = rows // PARTS
        at = pl.ds(piece * span, span)
        total = jnp.sum(acc_sum[0, at, :], axis=1, keepdims=True)
        x = blocks[me, at, :feat].astype(jnp.float32)
        out_vu[at, :] = acc_vu[0, at, :] * scale
        out_grad[at, :] = (acc_grad[0, at, :] - total * x) * scale
    for piece in range(PARTS):
        at = pl.ds(piece * span, span)
        result(piece).wait_recv()
        out_vu[at, :] += res_in[at, feat:].astype(jnp.float32) * scale
        out_grad[at, :] += res_in[at, :feat].astype(jnp.float32) * scale

    for piece in range(PARTS):
        result(piece).wait_send()
    for chunk in range(CHUNKS):
        copy(me, chunk, send_part.at[chunk], partner).wait_send()
    for t in range(2 * CHUNKS):
        chunk = t % CHUNKS
        plane = first if t < CHUNKS else second
        copy(slot_of(plane, y, c), chunk, send_side.at[t], side).wait_send()
        copy(slot_of(plane, y, c), chunk, send_sib.at[t], sib).wait_send()
        copy(slot_of(plane, 1 - y, c), chunk, send_sib.at[2 * CHUNKS + t], sib).wait_send()

    @pl.when(inner)
    def _():
        for chunk in range(CHUNKS):
            to_mid(chunk).wait_send()
            to_mid(CHUNKS + chunk).wait_send()


def paired_device(depth, points, left, right):
    rows, feat = points.shape
    wide = 2 * left.shape[1]
    bf, f32, dma = jnp.bfloat16, jnp.float32, pltpu.SemaphoreType.DMA
    return tuple(
        pl.pallas_call(
            functools.partial(paired_kernel, depth),
            out_shape=(
                jax.ShapeDtypeStruct((rows, wide), f32),
                jax.ShapeDtypeStruct((rows, feat), f32),
            ),
            in_specs=[pl.BlockSpec(memory_space=pltpu.VMEM)] * 3,
            out_specs=[pl.BlockSpec(memory_space=pltpu.VMEM)] * 2,
            scratch_shapes=[
                pltpu.VMEM((depth, rows, feat + wide), bf),
                pltpu.VMEM((2, rows, wide), bf),
                pltpu.VMEM((2, rows, 128), f32),
                pltpu.VMEM((2, rows, wide), f32),
                pltpu.VMEM((2, rows, feat), f32),
                pltpu.VMEM((2, rows, 128), f32),
                pltpu.VMEM((rows, feat + wide), bf),
                pltpu.VMEM((rows, feat + wide), bf),
                dma((depth * CHUNKS,)),
                dma((CHUNKS,)),
                dma((2 * CHUNKS,)),
                dma((4 * CHUNKS,)),
                dma((2 * CHUNKS,)),
                dma((PARTS,)),
                dma((PARTS,)),
            ],
            compiler_params=pltpu.CompilerParams(
                collective_id=0, has_side_effects=True, vmem_limit_bytes=48 * 2**20
            ),
        )(points, left, right)
    )


def gathered_kernel(depth, points, left, right, all_x, all_right, out_vu, out_grad, acc_sum):
    step = pl.program_id(0)
    feat = points.shape[1]
    half_log = math.log2(math.e) / feat
    scale = 1.0 / math.sqrt(points.shape[0] * depth)

    @pl.when(step == 0)
    def _():
        out_vu[...] = jnp.zeros_like(out_vu)
        out_grad[...] = jnp.zeros_like(out_grad)
        acc_sum[...] = jnp.zeros_like(acc_sum)

    own_left = jnp.concatenate([left[...], right[...]], axis=1)
    vu, grad, sums = pair_block(
        points[...], own_left, row_squares(points[...]) * half_log,
        all_x[...], all_right[...], column_squares(all_x[...]) * half_log,
    )
    out_vu[...] += vu
    out_grad[...] += grad
    acc_sum[...] += sums

    @pl.when(step == pl.num_programs(0) - 1)
    def _():
        total = jnp.sum(acc_sum[...], axis=1, keepdims=True)
        out_vu[...] = out_vu[...] * scale
        out_grad[...] = (out_grad[...] - total * points[...].astype(jnp.float32)) * scale


def gathered_device(depth, points, left, right):
    rows, feat = points.shape
    wide = 2 * left.shape[1]
    own_right = jnp.concatenate([right, left], axis=1)
    all_x = lax.all_gather(points, "blk", tiled=True)
    all_right = lax.all_gather(own_right, "blk", tiled=True)
    tile = 256

    def whole(array):
        return pl.BlockSpec(array.shape, lambda i: (0, 0))

    return tuple(
        pl.pallas_call(
            functools.partial(gathered_kernel, depth),
            grid=(rows * depth // tile,),
            out_shape=(
                jax.ShapeDtypeStruct((rows, wide), jnp.float32),
                jax.ShapeDtypeStruct((rows, feat), jnp.float32),
            ),
            in_specs=[
                whole(points), whole(left), whole(right),
                pl.BlockSpec((tile, feat), lambda i: (i, 0)),
                pl.BlockSpec((tile, wide), lambda i: (i, 0)),
            ],
            out_specs=[
                pl.BlockSpec((rows, wide), lambda i: (0, 0)),
                pl.BlockSpec((rows, feat), lambda i: (0, 0)),
            ],
            scratch_shapes=[pltpu.VMEM((rows, 128), jnp.float32)],
            compiler_params=pltpu.CompilerParams(vmem_limit_bytes=32 * 2**20),
        )(points, left, right, all_x, all_right)
    )


def solution(mesh):
    depth = mesh.shape["blk"]
    per_device = paired_device if depth == 16 else gathered_device
    spec = P(("groups", "blk"), None)
    return jax.shard_map(
        functools.partial(per_device, depth),
        mesh=mesh,
        in_specs=(spec, spec, spec),
        out_specs=(spec, spec),
        check_vma=False,
    )
```
